32 devices in a mesh: band: 2 (over y), row: 8 (over z, x), col: 2 (over core).
Axes of the slice: x: 2, y: 2, z: 4, core: 2. Of those that a mesh axis runs over, the one named last changes fastest.
Arguments:
- voltages: bfloat16 [4096, 161792], P(('band', 'row', 'col')), parts along dimension 0, may hold values from -6 to 6
- gains: float32 [4096, 32, 2], P(('band', 'row', 'col')), parts along dimension 0, may hold values from -4 to 4
Outputs:
- visibilities: bfloat16 [64, 2048, 2, 2048], P(('band', 'row'), None, None, 'col'), parts along dimension 0
The draws below stay inside these ranges and needn't reach their ends.
There are 2 independent parts, one for each index of `band`. The reference program is written for one: setup_inputs(seed, part) draws one part's arguments, and reference() takes and returns one part's arrays. A program takes and returns all parts, laid end to end along the dimension named above; each array names one. Nothing has to cross between parts.
All inputs are finite; a program needn't handle non-finite values.
Results may differ from the reference program's by a relative error of at most 0.0075.
Values may be sent and summed in bfloat16 or wider, within the bound.
A program may use at most 192 MiB of HBM per device.

```python
import math
import jax
import jax.numpy as jnp
from jax import lax

FEEDS = 2048
NFFT = 2048
TAPS = 16
CHANS = 32
SPECTRA = 64
FRAMES = 79
CHAN0 = 256
FEED_DEV = 128
SUB = 1
IBLOCK = 2048


def block_levels(rng, shape, split, least, largest):
    factor_of, own = 1.0, jax.random.fold_in(rng, 6)
    for position, shards_of in split:
        heights = jnp.exp(jax.random.uniform(jax.random.fold_in(own, position), (shards_of,), jnp.float32, least / len(split), largest / len(split)))
        factor_of = factor_of * jnp.repeat(heights, shape[position] // shards_of).reshape([-1 if axis == position else 1 for axis in range(len(shape))])
    return factor_of


def gaussian(key, shape, scale, limit, pieces=(), kind=jnp.bfloat16):
    values = jax.random.normal(key, shape, jnp.float32) * scale
    if len(pieces) > 0:
        values = block_levels(key, shape, pieces, -0.22, 0.18) * values
    return jnp.clip(values, min=-limit, max=limit).astype(kind)


def setup_inputs(seed: int = 0, part: int = 0) -> dict:
    arg_keys = jax.random.split(jax.random.key(seed), 3)
    own_keys = jax.random.split(jax.random.fold_in(arg_keys[2], part), 3)
    voltages = gaussian(own_keys[0], (FEEDS, FRAMES * NFFT), 1.0, 6.0, ((0, 16),))
    gains = gaussian(own_keys[1], (FEEDS, CHANS, 2), 0.8, 4.0, ((0, 16),), jnp.float32)
    return dict(voltages=voltages, gains=gains)


def prototype(taps, length):
    total = taps * length
    index = jnp.arange(total).astype(jnp.float32)
    offset = (index - (total - 1) / 2.0) / length
    window = 0.5 - 0.5 * jnp.cos(2.0 * math.pi * (index + 0.5) / total)
    return (jnp.sinc(offset) * window).reshape(taps, length)


def dft_table(length, chans, first):
    sample = jnp.arange(length).astype(jnp.int32)
    channel = (first + jnp.arange(chans)).astype(jnp.int32)
    phase = (sample[:, None] * channel[None, :]) % length
    angle = phase.astype(jnp.float32) * (2.0 * math.pi / length)
    return jnp.concatenate([jnp.cos(angle), -jnp.sin(angle)], axis=1).astype(jnp.bfloat16)


def reference(voltages, gains):
    window = prototype(TAPS, NFFT)
    table = dft_table(NFFT, CHANS, CHAN0)
    scale = float(NFFT) ** -0.5
    blocks = voltages.reshape(FEEDS // FEED_DEV, FEED_DEV, FRAMES, NFFT)

    def channelize(block):
        total = jnp.zeros((FEED_DEV, SPECTRA, NFFT), jnp.float32)
        for tap in range(TAPS):
            total = total + block[:, tap:tap + SPECTRA, :].astype(jnp.float32) * window[tap]
        filtered = total.astype(jnp.bfloat16)
        raw = jnp.dot(filtered.reshape(FEED_DEV * SPECTRA, NFFT), table, preferred_element_type=jnp.float32) * scale
        return raw.reshape(FEED_DEV, SPECTRA, 2 * CHANS)

    raw = lax.map(channelize, blocks).reshape(FEEDS, SPECTRA, 2 * CHANS)
    real_part = raw[:, :, :CHANS]
    imag_part = raw[:, :, CHANS:]
    gain_re = gains[:, None, :, 0]
    gain_im = gains[:, None, :, 1]
    out_re = gain_re * real_part - gain_im * imag_part
    out_im = gain_re * imag_part + gain_im * real_part
    stacked = jnp.stack([out_re, out_im], axis=0)
    spectra = jnp.transpose(stacked, (3, 1, 0, 2)).reshape(CHANS, FEEDS, 2 * SPECTRA).astype(jnp.bfloat16)

    def correlate(chan_rows):
        turned = jnp.concatenate([-chan_rows[:, SPECTRA:], chan_rows[:, :SPECTRA]], axis=1)
        right = jnp.concatenate([chan_rows, turned], axis=0)
        product = jnp.dot(chan_rows, right.T, preferred_element_type=jnp.float32) / SPECTRA
        return product.astype(jnp.bfloat16).reshape(FEEDS, 2, FEEDS)

    result = lax.map(correlate, spectra)
    return result.reshape(CHANS * SUB, IBLOCK, 2, FEEDS)
```

```python
import math

import jax
import jax.numpy as jnp
import ml_dtypes
import numpy as np
from jax import lax
from jax.experimental import pallas as pl
from jax.experimental.pallas import tpu as pltpu
from jax.sharding import PartitionSpec as P

FEEDS = 2048
NFFT = 2048
TAPS = 16
SPECTRA = 64
LANES = 128
STEP = 8
MXU = 256
MESH = pl.DeviceIdType.MESH


def prototype(taps, length):
    total = taps * length
    index = jnp.arange(total).astype(jnp.float32)
    offset = (index - (total - 1) / 2.0) / length
    window = 0.5 - 0.5 * jnp.cos(2.0 * math.pi * (index + 0.5) / total)
    return (jnp.sinc(offset) * window).reshape(taps, length)


def dft_table(length, chans, first):
    sample = jnp.arange(length)
    channel = first + jnp.arange(chans)
    phase = sample[:, None] * channel[None, :] % length
    angle = phase.astype(jnp.float32) * (2.0 * math.pi / length)
    return jnp.concatenate([jnp.cos(angle), -jnp.sin(angle)], axis=1).astype(jnp.bfloat16)


def plain_shards(voltages, gains):
    rows = lax.axis_size("row")
    cols = lax.axis_size("col")
    feed_dev = voltages.shape[0]
    chans = gains.shape[1]
    sub = max(1, rows // chans)
    pairs = chans * sub // rows
    iblock = FEEDS // sub
    jblock = FEEDS // cols
    window = prototype(TAPS, NFFT)
    table = dft_table(NFFT, chans, NFFT // 8)
    scale = float(NFFT) ** (-0.5)
    blocks = voltages.reshape(feed_dev, -1, NFFT)
    total = jnp.zeros((feed_dev, SPECTRA, NFFT), jnp.float32)
    for tap in range(TAPS):
        total = total + blocks[:, tap : tap + SPECTRA, :].astype(jnp.float32) * window[tap]
    filtered = total.astype(jnp.bfloat16)
    raw = (
        jnp.dot(
            filtered.reshape(feed_dev * SPECTRA, NFFT), table, preferred_element_type=jnp.float32
        )
        * scale
    )
    raw = raw.reshape(feed_dev, SPECTRA, 2 * chans)
    real_part = raw[:, :, :chans]
    imag_part = raw[:, :, chans:]
    gain_re = gains[:, None, :, 0]
    gain_im = gains[:, None, :, 1]
    out_re = gain_re * real_part - gain_im * imag_part
    out_im = gain_re * imag_part + gain_im * real_part
    stacked = jnp.stack([out_re, out_im], axis=0)
    spectra = (
        jnp.transpose(stacked, (3, 1, 0, 2))
        .reshape(chans, feed_dev, 2 * SPECTRA)
        .astype(jnp.bfloat16)
    )
    outgoing = jnp.repeat(spectra, sub, axis=0)
    turned = lax.all_to_all(outgoing, "row", split_axis=0, concat_axis=1, tiled=True)
    turned = turned.reshape(pairs, rows, feed_dev, 2 * SPECTRA)
    gathered = lax.all_gather(turned, "col", axis=2, tiled=True)
    gathered = gathered.reshape(pairs, FEEDS, 2 * SPECTRA)
    pair_index = lax.axis_index("row") * pairs + jnp.arange(pairs)
    starts = pair_index % sub * iblock

    def first_rows(chan_rows, start):
        return lax.dynamic_slice_in_dim(chan_rows, start, iblock, 0)

    left = jax.vmap(first_rows)(gathered, starts)
    second = lax.dynamic_slice_in_dim(gathered, lax.axis_index("col") * jblock, jblock, 1)
    turned_second = jnp.concatenate([-second[:, :, SPECTRA:], second[:, :, :SPECTRA]], axis=2)
    right = jnp.concatenate([second, turned_second], axis=1)
    product = jnp.einsum("pis,pjs->pij", left, right, preferred_element_type=jnp.float32) / SPECTRA
    return product.astype(jnp.bfloat16).reshape(pairs, iblock, 2, jblock)


def folded_weights(chans, first):
    total = TAPS * NFFT
    m = np.arange(total)
    h = np.sinc((m - (total - 1) / 2.0) / NFFT) * (
        0.5 - 0.5 * np.cos(2.0 * np.pi * (m + 0.5) / total)
    )
    h = h.reshape(TAPS, NFFT)[:, : NFFT // 2]
    n = np.arange(NFFT // 2) - (NFFT - 1) / 2.0
    angle = 2.0 * np.pi / NFFT * n[:, None] * (first + np.arange(chans))[None, :]
    cos, sin = np.cos(angle), np.sin(angle)
    even, odd = [], []
    for u in range(TAPS // 2):
        plus = 0.5 * (h[u] + h[TAPS - 1 - u])[:, None]
        minus = 0.5 * (h[u] - h[TAPS - 1 - u])[:, None]
        even += [plus * cos, -minus * sin]
        odd += [minus * cos, -plus * sin]
    return [np.concatenate(x, axis=1).astype(ml_dtypes.bfloat16) for x in (even, odd)]


def rotation(chans, first):
    phase = -2.0 * np.pi / NFFT * (NFFT - 1) / 2.0 * (first + np.arange(chans))
    scale = NFFT**-0.5 * SPECTRA**-0.5
    turn = np.stack([np.cos(phase), np.sin(phase)], axis=1) * scale
    return np.repeat(turn[:, :, None], LANES, axis=2).astype(np.float32)


def channelize_kernel(rows, pairs, *refs):
    frames = refs[:STEP]
    even_w, odd_w, flip, gains, turn, out, even, odd, low_acc, high_acc, stage, ready = refs[STEP : STEP + 12]
    send_sem, recv_sem, own_sem, pass_sem, passed_sem = refs[STEP + 12 :]
    i = pl.program_id(0)
    steps = pl.num_programs(0)
    feed_dev = frames[0].shape[0]
    half = NFFT // 2
    band, row, col = lax.axis_index("band"), lax.axis_index("row"), lax.axis_index("col")
    chunks = SPECTRA // STEP
    chans = rows * pairs
    delay = TAPS // STEP

    def to_row(ch, d):
        dest = lax.rem(row + d, rows)
        return pltpu.make_async_remote_copy(
            src_ref=ready.at[ch, pl.ds(dest * pairs, pairs)],
            dst_ref=out.at[:, row, col, pl.ds(pl.multiple_of(ch * 2 * STEP, 2 * STEP), 2 * STEP), :],
            send_sem=send_sem.at[ch, d],
            recv_sem=recv_sem.at[ch, d],
            device_id=(band, dest, col),
            device_id_type=MESH,
        )

    def from_row(ch, d):
        src = lax.rem(row + rows - d, rows)
        return pltpu.make_async_remote_copy(
            src_ref=ready.at[ch, pl.ds(src * pairs, pairs)],
            dst_ref=out.at[:, src, col, pl.ds(pl.multiple_of(ch * 2 * STEP, 2 * STEP), 2 * STEP), :],
            send_sem=send_sem.at[ch, d],
            recv_sem=recv_sem.at[ch, d],
            device_id=(band, src, col),
            device_id_type=MESH,
        )

    def own(ch):
        return pltpu.make_async_copy(
            ready.at[ch, pl.ds(row * pairs, pairs)],
            out.at[:, row, col, pl.ds(pl.multiple_of(ch * 2 * STEP, 2 * STEP), 2 * STEP), :],
            own_sem.at[ch],
        )

    def to_sibling(ch, c):
        block = out.at[:, :, c, pl.ds(pl.multiple_of(ch * 2 * STEP, 2 * STEP), 2 * STEP), :]
        return pltpu.make_async_remote_copy(
            src_ref=block,
            dst_ref=block,
            send_sem=pass_sem.at[ch],
            recv_sem=passed_sem.at[ch],
            device_id=(band, row, 1 - col),
            device_id_type=MESH,
        )

    def hand_on(ch):
        own(ch).wait()
        for d in range(1, rows):
            from_row(ch, d).wait_recv()
        to_sibling(ch, col).start()

    barrier = pltpu.get_barrier_semaphore()

    @pl.when(i == 0)
    def _():
        for d in range(1, rows):
            pl.semaphore_signal(
                barrier, inc=1, device_id=(band, lax.rem(row + d, rows), col), device_id_type=MESH
            )
        pl.semaphore_signal(barrier, inc=1, device_id=(band, row, 1 - col), device_id_type=MESH)
        low_acc[...] = jnp.zeros_like(low_acc)
        high_acc[...] = jnp.zeros_like(high_acc)

    for m in range(half // MXU):
        tail = jnp.concatenate(
            [f[:, NFFT - (m + 1) * MXU : NFFT - m * MXU] for f in frames], axis=0
        )
        tail = jnp.dot(tail, flip[...], preferred_element_type=jnp.float32).astype(jnp.bfloat16)
        head = jnp.concatenate([f[:, m * MXU : (m + 1) * MXU] for f in frames], axis=0)
        even[:, m * MXU : (m + 1) * MXU] = head + tail
        odd[:, m * MXU : (m + 1) * MXU] = head - tail

    for q in range(TAPS * chans // MXU):
        ge = jnp.dot(even[...], even_w[:, q * MXU : (q + 1) * MXU], preferred_element_type=jnp.float32)
        go = jnp.dot(odd[...], odd_w[:, q * MXU : (q + 1) * MXU], preferred_element_type=jnp.float32)
        low = ge + go
        high = ge - go
        for t in range(MXU // LANES):
            j = q * (MXU // LANES) + t
            cut = slice(t * LANES, (t + 1) * LANES)
            at = pl.ds(i * STEP + STEP - 2 - 2 * j, STEP)
            low_acc[at] += low[:, cut].reshape(STEP, feed_dev, LANES)
            at = pl.ds(i * STEP + 2 * j, STEP)
            high_acc[at] += high[:, cut].reshape(STEP, feed_dev, LANES)

    @pl.when(i == delay)
    def _():
        pl.semaphore_wait(barrier, rows)

    @pl.when(i >= delay)
    def _():
        ch = i - delay
        s0 = ch * STEP
        lane = lax.broadcasted_iota(jnp.int32, (feed_dev, LANES), 1)
        first = lane < LANES // 2
        sign = jnp.where(lax.rem(lane, 2 * chans) < chans, 1.0, -1.0).astype(jnp.float32)
        turn_re, turn_im = turn[:, 0, :], turn[:, 1, :]
        own_re, own_im = gains[:, 0, :], gains[:, 1, :]
        gain_re = own_re * turn_re - own_im * turn_im
        gain_im = own_re * turn_im + own_im * turn_re
        for s in range(0, STEP, 2):
            a = [low_acc[s0 + STEP - 1 + s + e] + sign * high_acc[s0 + 2 * STEP + s + e] for e in (0, 1)]
            b = [low_acc[s0 + STEP + s + e] + sign * high_acc[s0 + 2 * STEP - 1 + s + e] for e in (0, 1)]
            mine = jnp.where(first, a[0], b[1])
            other = jnp.where(first, a[1], b[0])
            both = (mine + pltpu.roll(other, LANES // 2, 1)).T
            for e in (0, 1):
                re = both[2 * chans * e : 2 * chans * e + chans]
                im = both[2 * chans * e + chans : 2 * chans * (e + 1)]
                stage[pl.ds(s + e, chans, stride=2 * STEP), :] = gain_re * re - gain_im * im
                stage[pl.ds(STEP + s + e, chans, stride=2 * STEP), :] = gain_re * im + gain_im * re
        ready[ch] = stage[...].reshape(chans, 2 * STEP, LANES).astype(jnp.bfloat16)
        for d in range(1, rows):
            to_row(ch, d).start()
        own(ch).start()

    @pl.when(i >= 2 * delay)
    def _():
        hand_on(i - 2 * delay)

    @pl.when(i == steps - 1)
    def _():
        for ch in range(chunks - delay, chunks):
            hand_on(ch)

        @pl.loop(0, chunks)
        def _(ch):
            for d in range(1, rows):
                to_row(ch, d).wait_send()
            to_sibling(ch, col).wait_send()
            to_sibling(ch, 1 - col).wait_recv()


def channelize(voltages, gains):
    rows = lax.axis_size("row")
    cols = lax.axis_size("col")
    feed_dev, samples = voltages.shape
    chans = gains.shape[1]
    pairs = chans // rows
    frames = samples // NFFT
    steps = (frames + 1) // STEP
    half = NFFT // 2
    chunks = SPECTRA // STEP
    even_w, odd_w = folded_weights(chans, NFFT // 8)
    flip = np.eye(MXU)[::-1].astype(ml_dtypes.bfloat16)
    turn = rotation(chans, NFFT // 8)

    def frame_spec(a):
        return pl.BlockSpec((feed_dev, NFFT), lambda i: (0, jnp.maximum(i * STEP + a - 1, 0)))

    def whole(shape):
        return pl.BlockSpec(shape, lambda i: (0,) * len(shape))

    depth = steps * STEP + STEP

    def kernel(*refs):
        channelize_kernel(rows, pairs, *refs)

    return pl.pallas_call(
        kernel,
        grid=(steps,),
        out_shape=jax.ShapeDtypeStruct((pairs, rows, cols, 2 * SPECTRA, feed_dev), jnp.bfloat16),
        in_specs=[frame_spec(a) for a in range(STEP)]
        + [whole(even_w.shape), whole(odd_w.shape), whole(flip.shape)]
        + [whole((chans, 2, feed_dev)), whole(turn.shape)],
        out_specs=pl.BlockSpec(memory_space=pl.ANY),
        scratch_shapes=[
            pltpu.VMEM((STEP * feed_dev, half), jnp.bfloat16),
            pltpu.VMEM((STEP * feed_dev, half), jnp.bfloat16),
            pltpu.VMEM((depth, feed_dev, LANES), jnp.float32),
            pltpu.VMEM((depth, feed_dev, LANES), jnp.float32),
            pltpu.VMEM((chans * 2 * STEP, LANES), jnp.float32),
            pltpu.VMEM((chunks, chans, 2 * STEP, LANES), jnp.bfloat16),
            pltpu.SemaphoreType.DMA((chunks, rows)),
            pltpu.SemaphoreType.DMA((chunks, rows)),
            pltpu.SemaphoreType.DMA((chunks,)),
            pltpu.SemaphoreType.DMA((chunks,)),
            pltpu.SemaphoreType.DMA((chunks,)),
        ],
        compiler_params=pltpu.CompilerParams(
            collective_id=0,
            has_side_effects=True,
            vmem_limit_bytes=56 << 20,
            dimension_semantics=("arbitrary",),
        ),
        name="channelize",
    )(
        *([voltages] * STEP),
        jnp.asarray(even_w),
        jnp.asarray(odd_w),
        jnp.asarray(flip),
        jnp.transpose(gains, (1, 2, 0)),
        jnp.asarray(turn),
    )


def correlate_kernel(spectra, out, mixed, held, sem):
    _, rows, cols, depth, feed_dev = spectra.shape
    c, q = pl.program_id(0), pl.program_id(1)
    nq = pl.num_programs(1)
    step = c * nq + q
    last = pl.num_programs(0) * nq - 1
    slot = lax.rem(step, 2)
    parts = held.shape[1]
    iblock = held.shape[2]
    jblocks = rows * cols // lax.axis_size("col")
    iblocks = iblock // feed_dev
    col = lax.axis_index("col")

    def put(st, jt):
        return pltpu.make_async_copy(
            held.at[lax.rem(st, 2), jt],
            out.at[
                lax.div(st, nq),
                pl.ds(lax.rem(st, nq) * iblock, iblock),
                :,
                pl.ds(jt * LANES, LANES),
            ],
            sem.at[lax.rem(st, 2), jt],
        )

    for b in range(iblocks):
        at = q * iblocks + b
        y = spectra[0, lax.div(at, cols), lax.rem(at, cols)].astype(jnp.float32)
        z = y.reshape(depth // (2 * STEP), 2, STEP, feed_dev)
        z = jnp.concatenate([z[:, 1:], -z[:, :1]], axis=1).reshape(depth, feed_dev)
        mixed[pl.ds(2 * b * feed_dev, feed_dev, stride=2), :] = y.T
        mixed[pl.ds(2 * b * feed_dev + 1, feed_dev, stride=2), :] = z.T
    left = mixed[...].astype(jnp.bfloat16)

    @pl.when(step >= 2)
    def _():
        for jt in range(parts):
            put(step - 2, jt).wait()

    wide = MXU // LANES
    for g in range(parts // wide):
        side = []
        for t in range(wide):
            at = col * jblocks + g * wide + t
            side.append(spectra[0, lax.div(at, cols), lax.rem(at, cols)])
        right = jnp.concatenate(side, axis=1)
        product = jnp.dot(left, right, preferred_element_type=jnp.float32).astype(jnp.bfloat16)
        for t in range(wide):
            jt = g * wide + t
            held.at[slot, jt].reshape(2 * iblock, LANES)[...] = product[:, t * LANES : (t + 1) * LANES]
            put(step, jt).start()

    @pl.when(step == last)
    def _():
        for st in (last - 1, last):
            for jt in range(parts):
                put(st, jt).wait()


def correlate(spectra):
    pairs, rows, cols, depth, feed_dev = spectra.shape
    jblock = FEEDS // cols
    iblock = 4 * feed_dev
    return pl.pallas_call(
        correlate_kernel,
        grid=(pairs, FEEDS // iblock),
        out_shape=jax.ShapeDtypeStruct((pairs, FEEDS, 2, jblock), jnp.bfloat16),
        in_specs=[pl.BlockSpec((1, rows, cols, depth, feed_dev), lambda c, q: (c, 0, 0, 0, 0))],
        out_specs=pl.BlockSpec(memory_space=pl.ANY),
        scratch_shapes=[
            pltpu.VMEM((2 * iblock, depth), jnp.float32),
            pltpu.VMEM((2, jblock // LANES, iblock, 2, LANES), jnp.bfloat16),
            pltpu.SemaphoreType.DMA((2, jblock // LANES)),
        ],
        compiler_params=pltpu.CompilerParams(
            vmem_limit_bytes=40 << 20, dimension_semantics=("arbitrary", "arbitrary")
        ),
        name="correlate",
    )(spectra)


def shards(voltages, gains):
    rows = lax.axis_size("row")
    cols = lax.axis_size("col")
    chans = gains.shape[1]
    fits = (
        voltages.shape[0] == LANES
        and rows * cols * LANES == FEEDS
        and cols == 2
        and chans % rows == 0
        and 4 * chans == LANES
        and voltages.shape[1] == (SPECTRA + TAPS - 1) * NFFT
    )
    if not fits:
        return plain_shards(voltages, gains)
    return correlate(channelize(voltages, gains))


def solution(mesh):
    placed = (P(("band", "row", "col"), None), P(("band", "row", "col"), None, None))
    return jax.shard_map(
        shards,
        mesh=mesh,
        in_specs=placed,
        out_specs=P(("band", "row"), None, None, "col"),
        check_vma=False,
    )
```

```python
import math

import jax
import jax.numpy as jnp
import ml_dtypes
import numpy as np
from jax import lax
from jax.experimental import pallas as pl
from jax.experimental.pallas import tpu as pltpu
from jax.sharding import PartitionSpec as P

FEEDS = 2048
NFFT = 2048
TAPS = 16
SPECTRA = 64
LANES = 128
STEP = 8
GROUP = 2
MXU = 256
PITCH = 17
MESH = pl.DeviceIdType.MESH


def prototype(taps, length):
    total = taps * length
    index = jnp.arange(total).astype(jnp.float32)
    offset = (index - (total - 1) / 2.0) / length
    window = 0.5 - 0.5 * jnp.cos(2.0 * math.pi * (index + 0.5) / total)
    return (jnp.sinc(offset) * window).reshape(taps, length)


def dft_table(length, chans, first):
    sample = jnp.arange(length)
    channel = first + jnp.arange(chans)
    phase = sample[:, None] * channel[None, :] % length
    angle = phase.astype(jnp.float32) * (2.0 * math.pi / length)
    return jnp.concatenate([jnp.cos(angle), -jnp.sin(angle)], axis=1).astype(jnp.bfloat16)


def plain_shards(voltages, gains):
    rows = lax.axis_size("row")
    cols = lax.axis_size("col")
    feed_dev = voltages.shape[0]
    chans = gains.shape[1]
    sub = max(1, rows // chans)
    pairs = chans * sub // rows
    iblock = FEEDS // sub
    jblock = FEEDS // cols
    window = prototype(TAPS, NFFT)
    table = dft_table(NFFT, chans, NFFT // 8)
    scale = float(NFFT) ** (-0.5)
    blocks = voltages.reshape(feed_dev, -1, NFFT)
    total = jnp.zeros((feed_dev, SPECTRA, NFFT), jnp.float32)
    for tap in range(TAPS):
        total = total + blocks[:, tap : tap + SPECTRA, :].astype(jnp.float32) * window[tap]
    filtered = total.astype(jnp.bfloat16)
    raw = (
        jnp.dot(
            filtered.reshape(feed_dev * SPECTRA, NFFT), table, preferred_element_type=jnp.float32
        )
        * scale
    )
    raw = raw.reshape(feed_dev, SPECTRA, 2 * chans)
    real_part = raw[:, :, :chans]
    imag_part = raw[:, :, chans:]
    gain_re = gains[:, None, :, 0]
    gain_im = gains[:, None, :, 1]
    out_re = gain_re * real_part - gain_im * imag_part
    out_im = gain_re * imag_part + gain_im * real_part
    stacked = jnp.stack([out_re, out_im], axis=0)
    spectra = (
        jnp.transpose(stacked, (3, 1, 0, 2))
        .reshape(chans, feed_dev, 2 * SPECTRA)
        .astype(jnp.bfloat16)
    )
    outgoing = jnp.repeat(spectra, sub, axis=0)
    turned = lax.all_to_all(outgoing, "row", split_axis=0, concat_axis=1, tiled=True)
    turned = turned.reshape(pairs, rows, feed_dev, 2 * SPECTRA)
    gathered = lax.all_gather(turned, "col", axis=2, tiled=True)
    gathered = gathered.reshape(pairs, FEEDS, 2 * SPECTRA)
    pair_index = lax.axis_index("row") * pairs + jnp.arange(pairs)
    starts = pair_index % sub * iblock

    def first_rows(chan_rows, start):
        return lax.dynamic_slice_in_dim(chan_rows, start, iblock, 0)

    left = jax.vmap(first_rows)(gathered, starts)
    second = lax.dynamic_slice_in_dim(gathered, lax.axis_index("col") * jblock, jblock, 1)
    turned_second = jnp.concatenate([-second[:, :, SPECTRA:], second[:, :, :SPECTRA]], axis=2)
    right = jnp.concatenate([second, turned_second], axis=1)
    product = jnp.einsum("pis,pjs->pij", left, right, preferred_element_type=jnp.float32) / SPECTRA
    return product.astype(jnp.bfloat16).reshape(pairs, iblock, 2, jblock)


def folded_weights(chans, first):
    total = TAPS * NFFT
    m = np.arange(total)
    h = np.sinc((m - (total - 1) / 2.0) / NFFT) * (
        0.5 - 0.5 * np.cos(2.0 * np.pi * (m + 0.5) / total)
    )
    h = h.reshape(TAPS, NFFT)[:, : NFFT // 2]
    n = np.arange(NFFT // 2) - (NFFT - 1) / 2.0
    angle = 2.0 * np.pi / NFFT * n[:, None] * (first + np.arange(chans))[None, :]
    cos, sin = np.cos(angle), np.sin(angle)
    even, odd = [], []
    for u in range(TAPS // 2):
        plus = 0.5 * (h[u] + h[TAPS - 1 - u])[:, None]
        minus = 0.5 * (h[u] - h[TAPS - 1 - u])[:, None]
        even += [plus * cos, -minus * sin]
        odd += [minus * cos, -plus * sin]
    return [np.concatenate(x, axis=1).astype(ml_dtypes.bfloat16) for x in (even, odd)]


def rotation(chans, first):
    phase = -2.0 * np.pi / NFFT * (NFFT - 1) / 2.0 * (first + np.arange(chans))
    scale = NFFT**-0.5 * SPECTRA**-0.5
    turn = np.stack([np.cos(phase), np.sin(phase)], axis=1) * scale
    return np.repeat(turn[:, :, None], LANES, axis=2).astype(np.float32)


def channelize_kernel(rows, pairs, *refs):
    frames = refs[:STEP]
    even_w, odd_w, flip, gains, turn, out, even, odd, low_acc, high_acc, stage, ready = refs[STEP : STEP + 12]
    send_sem, recv_sem, own_sem, pass_sem, passed_sem = refs[STEP + 12 :]
    i = pl.program_id(0)
    steps = pl.num_programs(0)
    feed_dev = frames[0].shape[0]
    half = NFFT // 2
    band, row, col = lax.axis_index("band"), lax.axis_index("row"), lax.axis_index("col")
    chunks = SPECTRA // STEP
    chans = rows * pairs
    delay = TAPS // STEP

    def to_row(ch, d):
        dest = lax.rem(row + d, rows)
        return pltpu.make_async_remote_copy(
            src_ref=ready.at[ch, pl.ds(dest * pairs, pairs)],
            dst_ref=out.at[:, row, col, pl.ds(pl.multiple_of(ch * 2 * STEP, 2 * STEP), 2 * STEP), :],
            send_sem=send_sem.at[ch, d],
            recv_sem=recv_sem.at[ch, d],
            device_id=(band, dest, col),
            device_id_type=MESH,
        )

    def from_row(ch, d):
        src = lax.rem(row + rows - d, rows)
        return pltpu.make_async_remote_copy(
            src_ref=ready.at[ch, pl.ds(src * pairs, pairs)],
            dst_ref=out.at[:, src, col, pl.ds(pl.multiple_of(ch * 2 * STEP, 2 * STEP), 2 * STEP), :],
            send_sem=send_sem.at[ch, d],
            recv_sem=recv_sem.at[ch, d],
            device_id=(band, src, col),
            device_id_type=MESH,
        )

    def own(ch):
        return pltpu.make_async_copy(
            ready.at[ch, pl.ds(row * pairs, pairs)],
            out.at[:, row, col, pl.ds(pl.multiple_of(ch * 2 * STEP, 2 * STEP), 2 * STEP), :],
            own_sem.at[ch],
        )

    def to_sibling(ch, c):
        block = out.at[:, :, c, pl.ds(pl.multiple_of(ch * 2 * STEP, 2 * STEP), 2 * STEP), :]
        return pltpu.make_async_remote_copy(
            src_ref=block,
            dst_ref=block,
            send_sem=pass_sem.at[ch],
            recv_sem=passed_sem.at[ch],
            device_id=(band, row, 1 - col),
            device_id_type=MESH,
        )

    def hand_on(ch):
        own(ch).wait()
        for d in range(1, rows):
            from_row(ch, d).wait_recv()
        to_sibling(ch, col).start()

    barrier = pltpu.get_barrier_semaphore()

    @pl.when(i == 0)
    def _():
        for d in range(1, rows):
            pl.semaphore_signal(
                barrier, inc=1, device_id=(band, lax.rem(row + d, rows), col), device_id_type=MESH
            )
        pl.semaphore_signal(barrier, inc=1, device_id=(band, row, 1 - col), device_id_type=MESH)
        low_acc[...] = jnp.zeros_like(low_acc)
        high_acc[...] = jnp.zeros_like(high_acc)

    for first in range(0, STEP, GROUP):
        group = frames[first : first + GROUP]
        span = slice(first * feed_dev, (first + GROUP) * feed_dev)
        for m in range(half // MXU):
            tail = jnp.concatenate(
                [f[:, NFFT - (m + 1) * MXU : NFFT - m * MXU] for f in group], axis=0
            )
            tail = jnp.dot(tail, flip[...], preferred_element_type=jnp.float32).astype(jnp.bfloat16)
            head = jnp.concatenate([f[:, m * MXU : (m + 1) * MXU] for f in group], axis=0)
            even[span, m * MXU : (m + 1) * MXU] = head + tail
            odd[span, m * MXU : (m + 1) * MXU] = head - tail

    for first in range(0, STEP, GROUP):
        span = slice(first * feed_dev, (first + GROUP) * feed_dev)
        for q in range(TAPS * chans // MXU):
            cols = slice(q * MXU, (q + 1) * MXU)
            ge = jnp.dot(even[span], even_w[:, cols], preferred_element_type=jnp.float32)
            go = jnp.dot(odd[span], odd_w[:, cols], preferred_element_type=jnp.float32)
            low = ge + go
            high = ge - go
            for t in range(MXU // LANES):
                j = q * (MXU // LANES) + t
                cut = slice(t * LANES, (t + 1) * LANES)
                at = pl.ds(i * STEP + STEP - 2 - 2 * j + first, GROUP)
                low_acc[at] += low[:, cut].reshape(GROUP, feed_dev, LANES)
                at = pl.ds(i * STEP + 2 * j + first, GROUP)
                high_acc[at] += high[:, cut].reshape(GROUP, feed_dev, LANES)

    @pl.when(i == delay)
    def _():
        pl.semaphore_wait(barrier, rows)

    @pl.when(i >= delay)
    def _():
        ch = i - delay
        s0 = ch * STEP
        lane = lax.broadcasted_iota(jnp.int32, (feed_dev, LANES), 1)
        first = lane < LANES // 2
        sign = jnp.where(lax.rem(lane, 2 * chans) < chans, 1.0, -1.0).astype(jnp.float32)
        turn_re, turn_im = turn[:, 0, :], turn[:, 1, :]
        own_re, own_im = gains[:, 0, :], gains[:, 1, :]
        gain_re = own_re * turn_re - own_im * turn_im
        gain_im = own_re * turn_im + own_im * turn_re
        for s in range(0, STEP, 2):
            a = [low_acc[s0 + STEP - 1 + s + e] + sign * high_acc[s0 + 2 * STEP + s + e] for e in (0, 1)]
            b = [low_acc[s0 + STEP + s + e] + sign * high_acc[s0 + 2 * STEP - 1 + s + e] for e in (0, 1)]
            mine = jnp.where(first, a[0], b[1])
            other = jnp.where(first, a[1], b[0])
            both = (mine + pltpu.roll(other, LANES // 2, 1)).T
            for e in (0, 1):
                re = both[2 * chans * e : 2 * chans * e + chans]
                im = both[2 * chans * e + chans : 2 * chans * (e + 1)]
                stage[pl.ds(s + e, chans, stride=2 * STEP), :] = gain_re * re - gain_im * im
                stage[pl.ds(STEP + s + e, chans, stride=2 * STEP), :] = gain_re * im + gain_im * re
        ready[ch] = stage[...].reshape(chans, 2 * STEP, LANES).astype(jnp.bfloat16)
        for d in range(1, rows):
            to_row(ch, d).start()
        own(ch).start()

    @pl.when(i >= 2 * delay)
    def _():
        hand_on(i - 2 * delay)

    @pl.when(i == steps - 1)
    def _():
        for ch in range(chunks - delay, chunks):
            hand_on(ch)

        @pl.loop(0, chunks)
        def _(ch):
            for d in range(1, rows):
                to_row(ch, d).wait_send()
            to_sibling(ch, col).wait_send()
            to_sibling(ch, 1 - col).wait_recv()


def channelize(voltages, gains):
    rows = lax.axis_size("row")
    cols = lax.axis_size("col")
    feed_dev, samples = voltages.shape
    chans = gains.shape[1]
    pairs = chans // rows
    frames = samples // NFFT
    steps = (frames + 1) // STEP
    half = NFFT // 2
    chunks = SPECTRA // STEP
    even_w, odd_w = folded_weights(chans, NFFT // 8)
    flip = np.eye(MXU)[::-1].astype(ml_dtypes.bfloat16)
    turn = rotation(chans, NFFT // 8)

    def frame_spec(a):
        return pl.BlockSpec((feed_dev, NFFT), lambda i: (0, jnp.maximum(i * STEP + a - 1, 0)))

    def whole(shape):
        return pl.BlockSpec(shape, lambda i: (0,) * len(shape))

    depth = steps * STEP + STEP

    def kernel(*refs):
        channelize_kernel(rows, pairs, *refs)

    return pl.pallas_call(
        kernel,
        grid=(steps,),
        out_shape=jax.ShapeDtypeStruct((pairs, rows, cols, 2 * SPECTRA, feed_dev), jnp.bfloat16),
        in_specs=[frame_spec(a) for a in range(STEP)]
        + [whole(even_w.shape), whole(odd_w.shape), whole(flip.shape)]
        + [whole((chans, 2, feed_dev)), whole(turn.shape)],
        out_specs=pl.BlockSpec(memory_space=pl.ANY),
        scratch_shapes=[
            pltpu.VMEM((STEP * feed_dev, half), jnp.bfloat16),
            pltpu.VMEM((STEP * feed_dev, half), jnp.bfloat16),
            pltpu.VMEM((depth, feed_dev, LANES), jnp.float32),
            pltpu.VMEM((depth, feed_dev, LANES), jnp.float32),
            pltpu.VMEM((chans * 2 * STEP, LANES), jnp.float32),
            pltpu.VMEM((chunks, chans, 2 * STEP, LANES), jnp.bfloat16),
            pltpu.SemaphoreType.DMA((chunks, rows)),
            pltpu.SemaphoreType.DMA((chunks, rows)),
            pltpu.SemaphoreType.DMA((chunks,)),
            pltpu.SemaphoreType.DMA((chunks,)),
            pltpu.SemaphoreType.DMA((chunks,)),
        ],
        compiler_params=pltpu.CompilerParams(
            collective_id=0,
            has_side_effects=True,
            vmem_limit_bytes=56 << 20,
            dimension_semantics=("arbitrary",),
        ),
        name="channelize",
    )(
        *([voltages] * STEP),
        jnp.asarray(even_w),
        jnp.asarray(odd_w),
        jnp.asarray(flip),
        jnp.transpose(gains, (1, 2, 0)),
        jnp.asarray(turn),
    )


def correlate_kernel(spectra, out, wide_rows):
    _, rows, cols, depth, feed_dev = spectra.shape
    q = pl.program_id(1)
    iblock = wide_rows.shape[0] // PITCH
    parts = out.shape[1] // iblock // 2
    jblocks = rows * cols // lax.axis_size("col")
    iblocks = iblock // feed_dev
    col = lax.axis_index("col")

    re_side, im_side = [], []
    for b in range(iblocks):
        at = q * iblocks + b
        y = spectra[0, lax.div(at, cols), lax.rem(at, cols)].astype(jnp.float32)
        z = y.reshape(depth // (2 * STEP), 2, STEP, feed_dev)
        z = jnp.concatenate([z[:, 1:], -z[:, :1]], axis=1).reshape(depth, feed_dev)
        re_side.append(y.T.astype(jnp.bfloat16))
        im_side.append(z.T.astype(jnp.bfloat16))
    lefts = [jnp.concatenate(x, axis=0) for x in (re_side, im_side)]

    wide = MXU // LANES
    for g in range(parts // wide):
        side = []
        for t in range(wide):
            at = col * jblocks + g * wide + t
            side.append(spectra[0, lax.div(at, cols), lax.rem(at, cols)])
        right = jnp.concatenate(side, axis=1)
        for p in (0, 1):
            product = jnp.dot(lefts[p], right, preferred_element_type=jnp.float32)
            for t in range(wide):
                at = 2 * (g * wide + t) + p
                wide_rows[pl.ds(at, iblock, stride=PITCH), :] = product[:, t * LANES : (t + 1) * LANES]

    @pl.loop(0, iblock, unroll=16)
    def _(r):
        rows_of = wide_rows[pl.ds(r * PITCH, 2 * parts), :]
        out[0, pl.ds(pl.multiple_of(r * 2 * parts, 2 * parts), 2 * parts), :] = rows_of.astype(jnp.bfloat16)


def correlate(spectra):
    pairs, rows, cols, depth, feed_dev = spectra.shape
    jblock = FEEDS // cols
    iblock = 4 * feed_dev
    parts = jblock // LANES
    flat = pl.pallas_call(
        correlate_kernel,
        grid=(pairs, FEEDS // iblock),
        out_shape=jax.ShapeDtypeStruct((pairs, FEEDS * 2 * parts, LANES), jnp.bfloat16),
        in_specs=[pl.BlockSpec((1, rows, cols, depth, feed_dev), lambda c, q: (c, 0, 0, 0, 0))],
        out_specs=pl.BlockSpec((1, iblock * 2 * parts, LANES), lambda c, q: (c, q, 0)),
        scratch_shapes=[pltpu.VMEM((iblock * PITCH, LANES), jnp.float32)],
        compiler_params=pltpu.CompilerParams(
            vmem_limit_bytes=63 << 20, dimension_semantics=("arbitrary", "arbitrary")
        ),
        name="correlate",
    )(spectra)
    flat = flat.reshape(pairs, FEEDS, parts, 2, LANES)
    return jnp.transpose(flat, (0, 1, 3, 2, 4)).reshape(pairs, FEEDS, 2, jblock)


def shards(voltages, gains):
    rows = lax.axis_size("row")
    cols = lax.axis_size("col")
    chans = gains.shape[1]
    fits = (
        voltages.shape[0] == LANES
        and rows * cols * LANES == FEEDS
        and cols == 2
        and FEEDS // cols // LANES == 8
        and chans % rows == 0
        and 4 * chans == LANES
        and voltages.shape[1] == (SPECTRA + TAPS - 1) * NFFT
    )
    if not fits:
        return plain_shards(voltages, gains)
    return correlate(channelize(voltages, gains))


def solution(mesh):
    placed = (P(("band", "row", "col"), None), P(("band", "row", "col"), None, None))
    return jax.shard_map(
        shards,
        mesh=mesh,
        in_specs=placed,
        out_specs=P(("band", "row"), None, None, "col"),
        check_vma=False,
    )
```

```python
import math

import jax
import jax.numpy as jnp
import ml_dtypes
import numpy as np
from jax import lax
from jax.experimental import pallas as pl
from jax.experimental.pallas import tpu as pltpu
from jax.sharding import PartitionSpec as P

FEEDS = 2048
NFFT = 2048
TAPS = 16
SPECTRA = 64
LANES = 128
STEP = 8
GROUP = 2
MXU = 256
PITCH = 17
MESH = pl.DeviceIdType.MESH


def prototype(taps, length):
    total = taps * length
    index = jnp.arange(total).astype(jnp.float32)
    offset = (index - (total - 1) / 2.0) / length
    window = 0.5 - 0.5 * jnp.cos(2.0 * math.pi * (index + 0.5) / total)
    return (jnp.sinc(offset) * window).reshape(taps, length)


def dft_table(length, chans, first):
    sample = jnp.arange(length)
    channel = first + jnp.arange(chans)
    phase = sample[:, None] * channel[None, :] % length
    angle = phase.astype(jnp.float32) * (2.0 * math.pi / length)
    return jnp.concatenate([jnp.cos(angle), -jnp.sin(angle)], axis=1).astype(jnp.bfloat16)


def plain_shards(voltages, gains):
    rows = lax.axis_size("row")
    cols = lax.axis_size("col")
    feed_dev = voltages.shape[0]
    chans = gains.shape[1]
    sub = max(1, rows // chans)
    pairs = chans * sub // rows
    iblock = FEEDS // sub
    jblock = FEEDS // cols
    window = prototype(TAPS, NFFT)
    table = dft_table(NFFT, chans, NFFT // 8)
    scale = float(NFFT) ** (-0.5)
    blocks = voltages.reshape(feed_dev, -1, NFFT)
    total = jnp.zeros((feed_dev, SPECTRA, NFFT), jnp.float32)
    for tap in range(TAPS):
        total = total + blocks[:, tap : tap + SPECTRA, :].astype(jnp.float32) * window[tap]
    filtered = total.astype(jnp.bfloat16)
    raw = (
        jnp.dot(
            filtered.reshape(feed_dev * SPECTRA, NFFT), table, preferred_element_type=jnp.float32
        )
        * scale
    )
    raw = raw.reshape(feed_dev, SPECTRA, 2 * chans)
    real_part = raw[:, :, :chans]
    imag_part = raw[:, :, chans:]
    gain_re = gains[:, None, :, 0]
    gain_im = gains[:, None, :, 1]
    out_re = gain_re * real_part - gain_im * imag_part
    out_im = gain_re * imag_part + gain_im * real_part
    stacked = jnp.stack([out_re, out_im], axis=0)
    spectra = (
        jnp.transpose(stacked, (3, 1, 0, 2))
        .reshape(chans, feed_dev, 2 * SPECTRA)
        .astype(jnp.bfloat16)
    )
    outgoing = jnp.repeat(spectra, sub, axis=0)
    turned = lax.all_to_all(outgoing, "row", split_axis=0, concat_axis=1, tiled=True)
    turned = turned.reshape(pairs, rows, feed_dev, 2 * SPECTRA)
    gathered = lax.all_gather(turned, "col", axis=2, tiled=True)
    gathered = gathered.reshape(pairs, FEEDS, 2 * SPECTRA)
    pair_index = lax.axis_index("row") * pairs + jnp.arange(pairs)
    starts = pair_index % sub * iblock

    def first_rows(chan_rows, start):
        return lax.dynamic_slice_in_dim(chan_rows, start, iblock, 0)

    left = jax.vmap(first_rows)(gathered, starts)
    second = lax.dynamic_slice_in_dim(gathered, lax.axis_index("col") * jblock, jblock, 1)
    turned_second = jnp.concatenate([-second[:, :, SPECTRA:], second[:, :, :SPECTRA]], axis=2)
    right = jnp.concatenate([second, turned_second], axis=1)
    product = jnp.einsum("pis,pjs->pij", left, right, preferred_element_type=jnp.float32) / SPECTRA
    return product.astype(jnp.bfloat16).reshape(pairs, iblock, 2, jblock)


def folded_weights(chans, first):
    total = TAPS * NFFT
    m = np.arange(total)
    h = np.sinc((m - (total - 1) / 2.0) / NFFT) * (
        0.5 - 0.5 * np.cos(2.0 * np.pi * (m + 0.5) / total)
    )
    h = h.reshape(TAPS, NFFT)[:, : NFFT // 2]
    n = np.arange(NFFT // 2) - (NFFT - 1) / 2.0
    angle = 2.0 * np.pi / NFFT * n[:, None] * (first + np.arange(chans))[None, :]
    cos, sin = np.cos(angle), np.sin(angle)
    even, odd = [], []
    for u in range(TAPS // 2):
        plus = 0.5 * (h[u] + h[TAPS - 1 - u])[:, None]
        minus = 0.5 * (h[u] - h[TAPS - 1 - u])[:, None]
        even += [plus * cos, -minus * sin]
        odd += [minus * cos, -plus * sin]
    return [np.concatenate(x, axis=1).astype(ml_dtypes.bfloat16) for x in (even, odd)]


def rotation(chans, first):
    phase = -2.0 * np.pi / NFFT * (NFFT - 1) / 2.0 * (first + np.arange(chans))
    scale = NFFT**-0.5 * SPECTRA**-0.5
    turn = np.stack([np.cos(phase), np.sin(phase)], axis=1) * scale
    return np.repeat(turn[:, :, None], LANES, axis=2).astype(np.float32)


def channelize_kernel(rows, pairs, *refs):
    frames = refs[:STEP]
    even_w, odd_w, gains, turn, out, even, odd, low_acc, high_acc, stage, ready = refs[STEP : STEP + 11]
    send_sem, recv_sem, own_sem, pass_sem, passed_sem = refs[STEP + 11 :]
    i = pl.program_id(0)
    steps = pl.num_programs(0)
    feed_dev = frames[0].shape[0]
    half = NFFT // 2
    band, row, col = lax.axis_index("band"), lax.axis_index("row"), lax.axis_index("col")
    chunks = SPECTRA // STEP
    chans = rows * pairs
    delay = TAPS // STEP

    def to_row(ch, d):
        dest = lax.rem(row + d, rows)
        return pltpu.make_async_remote_copy(
            src_ref=ready.at[ch, pl.ds(dest * pairs, pairs)],
            dst_ref=out.at[:, row, col, pl.ds(pl.multiple_of(ch * 2 * STEP, 2 * STEP), 2 * STEP), :],
            send_sem=send_sem.at[ch, d],
            recv_sem=recv_sem.at[ch, d],
            device_id=(band, dest, col),
            device_id_type=MESH,
        )

    def from_row(ch, d):
        src = lax.rem(row + rows - d, rows)
        return pltpu.make_async_remote_copy(
            src_ref=ready.at[ch, pl.ds(src * pairs, pairs)],
            dst_ref=out.at[:, src, col, pl.ds(pl.multiple_of(ch * 2 * STEP, 2 * STEP), 2 * STEP), :],
            send_sem=send_sem.at[ch, d],
            recv_sem=recv_sem.at[ch, d],
            device_id=(band, src, col),
            device_id_type=MESH,
        )

    def own(ch):
        return pltpu.make_async_copy(
            ready.at[ch, pl.ds(row * pairs, pairs)],
            out.at[:, row, col, pl.ds(pl.multiple_of(ch * 2 * STEP, 2 * STEP), 2 * STEP), :],
            own_sem.at[ch],
        )

    def to_sibling(ch, c):
        block = out.at[:, :, c, pl.ds(pl.multiple_of(ch * 2 * STEP, 2 * STEP), 2 * STEP), :]
        return pltpu.make_async_remote_copy(
            src_ref=block,
            dst_ref=block,
            send_sem=pass_sem.at[ch],
            recv_sem=passed_sem.at[ch],
            device_id=(band, row, 1 - col),
            device_id_type=MESH,
        )

    def hand_on(ch):
        own(ch).wait()
        for d in range(1, rows):
            from_row(ch, d).wait_recv()
        to_sibling(ch, col).start()

    barrier = pltpu.get_barrier_semaphore()

    @pl.when(i == 0)
    def _():
        for d in range(1, rows):
            pl.semaphore_signal(
                barrier, inc=1, device_id=(band, lax.rem(row + d, rows), col), device_id_type=MESH
            )
        pl.semaphore_signal(barrier, inc=1, device_id=(band, row, 1 - col), device_id_type=MESH)
        low_acc[...] = jnp.zeros_like(low_acc)
        high_acc[...] = jnp.zeros_like(high_acc)

    back = LANES - 1 - lax.broadcasted_iota(jnp.int32, (GROUP * feed_dev, LANES), 1)
    for first in range(0, STEP, GROUP):
        group = frames[first : first + GROUP]
        span = slice(first * feed_dev, (first + GROUP) * feed_dev)
        for m in range(half // LANES):
            tail = jnp.concatenate(
                [f[:, NFFT - (m + 1) * LANES : NFFT - m * LANES] for f in group], axis=0
            ).astype(jnp.float32)
            tail = jnp.take_along_axis(tail, back, axis=1, mode="promise_in_bounds")
            tail = tail.astype(jnp.bfloat16)
            head = jnp.concatenate([f[:, m * LANES : (m + 1) * LANES] for f in group], axis=0)
            even[span, m * LANES : (m + 1) * LANES] = head + tail
            odd[span, m * LANES : (m + 1) * LANES] = head - tail

    for first in range(0, STEP, GROUP):
        span = slice(first * feed_dev, (first + GROUP) * feed_dev)
        for q in range(TAPS * chans // MXU):
            cols = slice(q * MXU, (q + 1) * MXU)
            ge = jnp.dot(even[span], even_w[:, cols], preferred_element_type=jnp.float32)
            go = jnp.dot(odd[span], odd_w[:, cols], preferred_element_type=jnp.float32)
            low = ge + go
            high = ge - go
            for t in range(MXU // LANES):
                j = q * (MXU // LANES) + t
                cut = slice(t * LANES, (t + 1) * LANES)
                at = pl.ds(i * STEP + STEP - 2 - 2 * j + first, GROUP)
                low_acc[at] += low[:, cut].reshape(GROUP, feed_dev, LANES)
                at = pl.ds(i * STEP + 2 * j + first, GROUP)
                high_acc[at] += high[:, cut].reshape(GROUP, feed_dev, LANES)

    @pl.when(i == delay)
    def _():
        pl.semaphore_wait(barrier, rows)

    @pl.when(i >= delay)
    def _():
        ch = i - delay
        s0 = ch * STEP
        lane = lax.broadcasted_iota(jnp.int32, (feed_dev, LANES), 1)
        first = lane < LANES // 2
        sign = jnp.where(lax.rem(lane, 2 * chans) < chans, 1.0, -1.0).astype(jnp.float32)
        turn_re, turn_im = turn[:, 0, :], turn[:, 1, :]
        own_re, own_im = gains[:, 0, :], gains[:, 1, :]
        gain_re = own_re * turn_re - own_im * turn_im
        gain_im = own_re * turn_im + own_im * turn_re
        for s in range(0, STEP, 2):
            a = [low_acc[s0 + STEP - 1 + s + e] + sign * high_acc[s0 + 2 * STEP + s + e] for e in (0, 1)]
            b = [low_acc[s0 + STEP + s + e] + sign * high_acc[s0 + 2 * STEP - 1 + s + e] for e in (0, 1)]
            mine = jnp.where(first, a[0], b[1])
            other = jnp.where(first, a[1], b[0])
            both = (mine + pltpu.roll(other, LANES // 2, 1)).T
            for e in (0, 1):
                re = both[2 * chans * e : 2 * chans * e + chans]
                im = both[2 * chans * e + chans : 2 * chans * (e + 1)]
                stage[pl.ds(s + e, chans, stride=2 * STEP), :] = gain_re * re - gain_im * im
                stage[pl.ds(STEP + s + e, chans, stride=2 * STEP), :] = gain_re * im + gain_im * re
        ready[ch] = stage[...].reshape(chans, 2 * STEP, LANES).astype(jnp.bfloat16)
        for d in range(1, rows):
            to_row(ch, d).start()
        own(ch).start()

    @pl.when(i >= 2 * delay)
    def _():
        hand_on(i - 2 * delay)

    @pl.when(i == steps - 1)
    def _():
        for ch in range(chunks - delay, chunks):
            hand_on(ch)

        @pl.loop(0, chunks)
        def _(ch):
            for d in range(1, rows):
                to_row(ch, d).wait_send()
            to_sibling(ch, col).wait_send()
            to_sibling(ch, 1 - col).wait_recv()


def channelize(voltages, gains):
    rows = lax.axis_size("row")
    cols = lax.axis_size("col")
    feed_dev, samples = voltages.shape
    chans = gains.shape[1]
    pairs = chans // rows
    frames = samples // NFFT
    steps = (frames + 1) // STEP
    half = NFFT // 2
    chunks = SPECTRA // STEP
    even_w, odd_w = folded_weights(chans, NFFT // 8)
    turn = rotation(chans, NFFT // 8)

    def frame_spec(a):
        return pl.BlockSpec((feed_dev, NFFT), lambda i: (0, jnp.maximum(i * STEP + a - 1, 0)))

    def whole(shape):
        return pl.BlockSpec(shape, lambda i: (0,) * len(shape))

    depth = steps * STEP + STEP

    def kernel(*refs):
        channelize_kernel(rows, pairs, *refs)

    return pl.pallas_call(
        kernel,
        grid=(steps,),
        out_shape=jax.ShapeDtypeStruct((pairs, rows, cols, 2 * SPECTRA, feed_dev), jnp.bfloat16),
        in_specs=[frame_spec(a) for a in range(STEP)]
        + [whole(even_w.shape), whole(odd_w.shape)]
        + [whole((chans, 2, feed_dev)), whole(turn.shape)],
        out_specs=pl.BlockSpec(memory_space=pl.ANY),
        scratch_shapes=[
            pltpu.VMEM((STEP * feed_dev, half), jnp.bfloat16),
            pltpu.VMEM((STEP * feed_dev, half), jnp.bfloat16),
            pltpu.VMEM((depth, feed_dev, LANES), jnp.float32),
            pltpu.VMEM((depth, feed_dev, LANES), jnp.float32),
            pltpu.VMEM((chans * 2 * STEP, LANES), jnp.float32),
            pltpu.VMEM((chunks, chans, 2 * STEP, LANES), jnp.bfloat16),
            pltpu.SemaphoreType.DMA((chunks, rows)),
            pltpu.SemaphoreType.DMA((chunks, rows)),
            pltpu.SemaphoreType.DMA((chunks,)),
            pltpu.SemaphoreType.DMA((chunks,)),
            pltpu.SemaphoreType.DMA((chunks,)),
        ],
        compiler_params=pltpu.CompilerParams(
            collective_id=0,
            has_side_effects=True,
            vmem_limit_bytes=56 << 20,
            dimension_semantics=("arbitrary",),
        ),
        name="channelize",
    )(
        *([voltages] * STEP),
        jnp.asarray(even_w),
        jnp.asarray(odd_w),
        jnp.transpose(gains, (1, 2, 0)),
        jnp.asarray(turn),
    )


def correlate_kernel(spectra, out, wide_rows):
    _, rows, cols, depth, feed_dev = spectra.shape
    nq = FEEDS // (wide_rows.shape[1] // PITCH)
    step = jnp.minimum(pl.program_id(0), pl.num_programs(0) - 2)
    q = lax.rem(step, nq)
    slot = lax.rem(pl.program_id(0), 2)
    iblock = wide_rows.shape[1] // PITCH
    parts = out.shape[1] // iblock // 2
    jblocks = rows * cols // lax.axis_size("col")
    iblocks = iblock // feed_dev
    col = lax.axis_index("col")
    wide = MXU // LANES

    lefts = []
    for b in range(iblocks):
        at = q * iblocks + b
        y = spectra[0, lax.div(at, cols), lax.rem(at, cols)].astype(jnp.float32)
        z = y.reshape(depth // (2 * STEP), 2, STEP, feed_dev)
        z = jnp.concatenate([z[:, 1:], -z[:, :1]], axis=1).reshape(depth, feed_dev)
        lefts.append([y.T.astype(jnp.bfloat16), z.T.astype(jnp.bfloat16)])
    lefts = [jnp.concatenate(x, axis=0) for x in zip(*lefts)]
    rights = []
    for g in range(parts // wide):
        side = []
        for t in range(wide):
            at = col * jblocks + g * wide + t
            side.append(spectra[0, lax.div(at, cols), lax.rem(at, cols)])
        rights.append(jnp.concatenate(side, axis=1))

    pieces = 2 * (parts // wide)
    share = iblock // pieces
    for g in range(parts // wide):
        for p in (0, 1):
            product = jnp.dot(lefts[p], rights[g], preferred_element_type=jnp.float32)
            for t in range(wide):
                at = 2 * (g * wide + t) + p
                cut = product[:, t * LANES : (t + 1) * LANES]
                wide_rows[slot, pl.ds(at, iblock, stride=PITCH), :] = cut
            for r in range((2 * g + p) * share, (2 * g + p + 1) * share):
                rows_of = wide_rows[1 - slot, pl.ds(r * PITCH + lax.div(q, nq), 2 * parts), :]
                out[0, r * 2 * parts : (r + 1) * 2 * parts, :] = rows_of.astype(jnp.bfloat16)


def correlate(spectra):
    pairs, rows, cols, depth, feed_dev = spectra.shape
    jblock = FEEDS // cols
    iblock = 4 * feed_dev
    parts = jblock // LANES
    nq = FEEDS // iblock
    steps = pairs * nq

    def taken(n):
        return (jnp.minimum(n, steps - 1) // nq, 0, 0, 0, 0)

    def given(n):
        before = jnp.maximum(n - 1, 0)
        return (before // nq, before % nq, 0)

    flat = pl.pallas_call(
        correlate_kernel,
        grid=(steps + 1,),
        out_shape=jax.ShapeDtypeStruct((pairs, FEEDS * 2 * parts, LANES), jnp.bfloat16),
        in_specs=[pl.BlockSpec((1, rows, cols, depth, feed_dev), taken)],
        out_specs=pl.BlockSpec((1, iblock * 2 * parts, LANES), given),
        scratch_shapes=[pltpu.VMEM((2, iblock * PITCH, LANES), jnp.float32)],
        compiler_params=pltpu.CompilerParams(
            vmem_limit_bytes=63 << 20, dimension_semantics=("arbitrary",)
        ),
        name="correlate",
    )(spectra)
    flat = flat.reshape(pairs, FEEDS, parts, 2, LANES)
    return jnp.transpose(flat, (0, 1, 3, 2, 4)).reshape(pairs, FEEDS, 2, jblock)


def shards(voltages, gains):
    rows = lax.axis_size("row")
    cols = lax.axis_size("col")
    chans = gains.shape[1]
    fits = (
        voltages.shape[0] == LANES
        and rows * cols * LANES == FEEDS
        and cols == 2
        and FEEDS // cols // LANES == 8
        and chans % rows == 0
        and 4 * chans == LANES
        and voltages.shape[1] == (SPECTRA + TAPS - 1) * NFFT
    )
    if not fits:
        return plain_shards(voltages, gains)
    return correlate(channelize(voltages, gains))


def solution(mesh):
    placed = (P(("band", "row", "col"), None), P(("band", "row", "col"), None, None))
    return jax.shard_map(
        shards,
        mesh=mesh,
        in_specs=placed,
        out_specs=P(("band", "row"), None, None, "col"),
        check_vma=False,
    )
```

```python
import math

import jax
import jax.numpy as jnp
import ml_dtypes
import numpy as np
from jax import lax
from jax.experimental import pallas as pl
from jax.experimental.pallas import tpu as pltpu
from jax.sharding import PartitionSpec as P

FEEDS = 2048
NFFT = 2048
TAPS = 16
SPECTRA = 64
LANES = 128
STEP = 8
GROUP = 2
LAG = 3
MXU = 256
PITCH = 17
MESH = pl.DeviceIdType.MESH


def prototype(taps, length):
    total = taps * length
    index = jnp.arange(total).astype(jnp.float32)
    offset = (index - (total - 1) / 2.0) / length
    window = 0.5 - 0.5 * jnp.cos(2.0 * math.pi * (index + 0.5) / total)
    return (jnp.sinc(offset) * window).reshape(taps, length)


def dft_table(length, chans, first):
    sample = jnp.arange(length)
    channel = first + jnp.arange(chans)
    phase = sample[:, None] * channel[None, :] % length
    angle = phase.astype(jnp.float32) * (2.0 * math.pi / length)
    return jnp.concatenate([jnp.cos(angle), -jnp.sin(angle)], axis=1).astype(jnp.bfloat16)


def plain_shards(voltages, gains):
    rows = lax.axis_size("row")
    cols = lax.axis_size("col")
    feed_dev = voltages.shape[0]
    chans = gains.shape[1]
    sub = max(1, rows // chans)
    pairs = chans * sub // rows
    iblock = FEEDS // sub
    jblock = FEEDS // cols
    window = prototype(TAPS, NFFT)
    table = dft_table(NFFT, chans, NFFT // 8)
    scale = float(NFFT) ** (-0.5)
    blocks = voltages.reshape(feed_dev, -1, NFFT)
    total = jnp.zeros((feed_dev, SPECTRA, NFFT), jnp.float32)
    for tap in range(TAPS):
        total = total + blocks[:, tap : tap + SPECTRA, :].astype(jnp.float32) * window[tap]
    filtered = total.astype(jnp.bfloat16)
    raw = (
        jnp.dot(
            filtered.reshape(feed_dev * SPECTRA, NFFT), table, preferred_element_type=jnp.float32
        )
        * scale
    )
    raw = raw.reshape(feed_dev, SPECTRA, 2 * chans)
    real_part = raw[:, :, :chans]
    imag_part = raw[:, :, chans:]
    gain_re = gains[:, None, :, 0]
    gain_im = gains[:, None, :, 1]
    out_re = gain_re * real_part - gain_im * imag_part
    out_im = gain_re * imag_part + gain_im * real_part
    stacked = jnp.stack([out_re, out_im], axis=0)
    spectra = (
        jnp.transpose(stacked, (3, 1, 0, 2))
        .reshape(chans, feed_dev, 2 * SPECTRA)
        .astype(jnp.bfloat16)
    )
    outgoing = jnp.repeat(spectra, sub, axis=0)
    turned = lax.all_to_all(outgoing, "row", split_axis=0, concat_axis=1, tiled=True)
    turned = turned.reshape(pairs, rows, feed_dev, 2 * SPECTRA)
    gathered = lax.all_gather(turned, "col", axis=2, tiled=True)
    gathered = gathered.reshape(pairs, FEEDS, 2 * SPECTRA)
    pair_index = lax.axis_index("row") * pairs + jnp.arange(pairs)
    starts = pair_index % sub * iblock

    def first_rows(chan_rows, start):
        return lax.dynamic_slice_in_dim(chan_rows, start, iblock, 0)

    left = jax.vmap(first_rows)(gathered, starts)
    second = lax.dynamic_slice_in_dim(gathered, lax.axis_index("col") * jblock, jblock, 1)
    turned_second = jnp.concatenate([-second[:, :, SPECTRA:], second[:, :, :SPECTRA]], axis=2)
    right = jnp.concatenate([second, turned_second], axis=1)
    product = jnp.einsum("pis,pjs->pij", left, right, preferred_element_type=jnp.float32) / SPECTRA
    return product.astype(jnp.bfloat16).reshape(pairs, iblock, 2, jblock)


def folded_weights(chans, first):
    total = TAPS * NFFT
    m = np.arange(total)
    h = np.sinc((m - (total - 1) / 2.0) / NFFT) * (
        0.5 - 0.5 * np.cos(2.0 * np.pi * (m + 0.5) / total)
    )
    h = h.reshape(TAPS, NFFT)[:, : NFFT // 2]
    n = np.arange(NFFT // 2) - (NFFT - 1) / 2.0
    angle = 2.0 * np.pi / NFFT * n[:, None] * (first + np.arange(chans))[None, :]
    cos, sin = np.cos(angle), np.sin(angle)
    even, odd = [], []
    for u in range(TAPS // 2):
        plus = 0.5 * (h[u] + h[TAPS - 1 - u])[:, None]
        minus = 0.5 * (h[u] - h[TAPS - 1 - u])[:, None]
        even += [plus * cos, -minus * sin]
        odd += [minus * cos, -plus * sin]
    return [np.concatenate(x, axis=1).astype(ml_dtypes.bfloat16) for x in (even, odd)]


def rotation(chans, first):
    phase = -2.0 * np.pi / NFFT * (NFFT - 1) / 2.0 * (first + np.arange(chans))
    scale = NFFT**-0.5 * SPECTRA**-0.5
    turn = np.stack([np.cos(phase), np.sin(phase)], axis=1) * scale
    return np.repeat(turn[:, :, None], LANES, axis=2).astype(np.float32)


def channelize_kernel(rows, pairs, *refs):
    frames = refs[:STEP]
    even_w, odd_w, gains, turn, out, even, odd, low_acc, high_acc, stage, ready = refs[STEP : STEP + 11]
    send_sem, recv_sem, own_sem, pass_sem, passed_sem = refs[STEP + 11 :]
    i = pl.program_id(0)
    steps = pl.num_programs(0)
    feed_dev = frames[0].shape[0]
    half = NFFT // 2
    band, row, col = lax.axis_index("band"), lax.axis_index("row"), lax.axis_index("col")
    chunks = SPECTRA // STEP
    chans = rows * pairs
    delay = TAPS // STEP

    def to_row(ch, d):
        dest = lax.rem(row + d, rows)
        return pltpu.make_async_remote_copy(
            src_ref=ready.at[ch, pl.ds(dest * pairs, pairs)],
            dst_ref=out.at[:, row, col, pl.ds(pl.multiple_of(ch * 2 * STEP, 2 * STEP), 2 * STEP), :],
            send_sem=send_sem.at[ch, d],
            recv_sem=recv_sem.at[ch, d],
            device_id=(band, dest, col),
            device_id_type=MESH,
        )

    def from_row(ch, d):
        src = lax.rem(row + rows - d, rows)
        return pltpu.make_async_remote_copy(
            src_ref=ready.at[ch, pl.ds(src * pairs, pairs)],
            dst_ref=out.at[:, src, col, pl.ds(pl.multiple_of(ch * 2 * STEP, 2 * STEP), 2 * STEP), :],
            send_sem=send_sem.at[ch, d],
            recv_sem=recv_sem.at[ch, d],
            device_id=(band, src, col),
            device_id_type=MESH,
        )

    def own(ch):
        return pltpu.make_async_copy(
            ready.at[ch, pl.ds(row * pairs, pairs)],
            out.at[:, row, col, pl.ds(pl.multiple_of(ch * 2 * STEP, 2 * STEP), 2 * STEP), :],
            own_sem.at[ch],
        )

    def to_sibling(ch, c):
        block = out.at[:, :, c, pl.ds(pl.multiple_of(ch * 2 * STEP, 2 * STEP), 2 * STEP), :]
        return pltpu.make_async_remote_copy(
            src_ref=block,
            dst_ref=block,
            send_sem=pass_sem.at[ch],
            recv_sem=passed_sem.at[ch],
            device_id=(band, row, 1 - col),
            device_id_type=MESH,
        )

    def hand_on(ch):
        own(ch).wait()
        for d in range(1, rows):
            from_row(ch, d).wait_recv()
        to_sibling(ch, col).start()

    barrier = pltpu.get_barrier_semaphore()

    @pl.when(i == 0)
    def _():
        for d in range(1, rows):
            pl.semaphore_signal(
                barrier, inc=1, device_id=(band, lax.rem(row + d, rows), col), device_id_type=MESH
            )
        pl.semaphore_signal(barrier, inc=1, device_id=(band, row, 1 - col), device_id_type=MESH)
        low_acc[...] = jnp.zeros_like(low_acc)
        high_acc[...] = jnp.zeros_like(high_acc)

    back = LANES - 1 - lax.broadcasted_iota(jnp.int32, (GROUP * feed_dev, LANES), 1)

    def fold(first):
        group = frames[first : first + GROUP]
        span = slice(first * feed_dev, (first + GROUP) * feed_dev)
        for m in range(half // LANES):
            tail = jnp.concatenate(
                [f[:, NFFT - (m + 1) * LANES : NFFT - m * LANES] for f in group], axis=0
            ).astype(jnp.float32)
            tail = jnp.take_along_axis(tail, back, axis=1, mode="promise_in_bounds")
            tail = tail.astype(jnp.bfloat16)
            head = jnp.concatenate([f[:, m * LANES : (m + 1) * LANES] for f in group], axis=0)
            even[span, m * LANES : (m + 1) * LANES] = head + tail
            odd[span, m * LANES : (m + 1) * LANES] = head - tail

    fold(0)
    for first in range(0, STEP, GROUP):
        span = slice(first * feed_dev, (first + GROUP) * feed_dev)
        for q in range(TAPS * chans // MXU):
            cols = slice(q * MXU, (q + 1) * MXU)
            ge = jnp.dot(even[span], even_w[:, cols], preferred_element_type=jnp.float32)
            go = jnp.dot(odd[span], odd_w[:, cols], preferred_element_type=jnp.float32)
            if q == 0 and first + GROUP < STEP:
                fold(first + GROUP)
            low = ge + go
            high = ge - go
            for t in range(MXU // LANES):
                j = q * (MXU // LANES) + t
                cut = slice(t * LANES, (t + 1) * LANES)
                at = pl.ds(i * STEP + STEP - 2 - 2 * j + first, GROUP)
                low_acc[at] += low[:, cut].reshape(GROUP, feed_dev, LANES)
                at = pl.ds(i * STEP + 2 * j + first, GROUP)
                high_acc[at] += high[:, cut].reshape(GROUP, feed_dev, LANES)

    @pl.when(i == delay)
    def _():
        pl.semaphore_wait(barrier, rows)

    @pl.when(i >= delay)
    def _():
        ch = i - delay
        s0 = ch * STEP
        lane = lax.broadcasted_iota(jnp.int32, (feed_dev, LANES), 1)
        first = lane < LANES // 2
        sign = jnp.where(lax.rem(lane, 2 * chans) < chans, 1.0, -1.0).astype(jnp.float32)
        turn_re, turn_im = turn[:, 0, :], turn[:, 1, :]
        own_re, own_im = gains[:, 0, :], gains[:, 1, :]
        gain_re = own_re * turn_re - own_im * turn_im
        gain_im = own_re * turn_im + own_im * turn_re
        for s in range(0, STEP, 2):
            a = [low_acc[s0 + STEP - 1 + s + e] + sign * high_acc[s0 + 2 * STEP + s + e] for e in (0, 1)]
            b = [low_acc[s0 + STEP + s + e] + sign * high_acc[s0 + 2 * STEP - 1 + s + e] for e in (0, 1)]
            mine = jnp.where(first, a[0], b[1])
            other = jnp.where(first, a[1], b[0])
            both = (mine + pltpu.roll(other, LANES // 2, 1)).T
            for e in (0, 1):
                re = both[2 * chans * e : 2 * chans * e + chans]
                im = both[2 * chans * e + chans : 2 * chans * (e + 1)]
                stage[pl.ds(s + e, chans, stride=2 * STEP), :] = gain_re * re - gain_im * im
                stage[pl.ds(STEP + s + e, chans, stride=2 * STEP), :] = gain_re * im + gain_im * re
        ready[ch] = stage[...].reshape(chans, 2 * STEP, LANES).astype(jnp.bfloat16)
        for k in range(rows - 1):
            to_row(ch, 1 + lax.rem(k + 2 * row, rows - 1)).start()
        own(ch).start()

    @pl.when(i >= delay + LAG)
    def _():
        hand_on(i - delay - LAG)

    @pl.when(i == steps - 1)
    def _():
        for ch in range(chunks - LAG, chunks):
            hand_on(ch)

        @pl.loop(0, chunks)
        def _(ch):
            for d in range(1, rows):
                to_row(ch, d).wait_send()
            to_sibling(ch, col).wait_send()
            to_sibling(ch, 1 - col).wait_recv()


def channelize(voltages, gains):
    rows = lax.axis_size("row")
    cols = lax.axis_size("col")
    feed_dev, samples = voltages.shape
    chans = gains.shape[1]
    pairs = chans // rows
    frames = samples // NFFT
    steps = (frames + 1) // STEP
    half = NFFT // 2
    chunks = SPECTRA // STEP
    even_w, odd_w = folded_weights(chans, NFFT // 8)
    turn = rotation(chans, NFFT // 8)

    def frame_spec(a):
        return pl.BlockSpec((feed_dev, NFFT), lambda i: (0, jnp.maximum(i * STEP + a - 1, 0)))

    def whole(shape):
        return pl.BlockSpec(shape, lambda i: (0,) * len(shape))

    depth = steps * STEP + STEP

    def kernel(*refs):
        channelize_kernel(rows, pairs, *refs)

    return pl.pallas_call(
        kernel,
        grid=(steps,),
        out_shape=jax.ShapeDtypeStruct((pairs, rows, cols, 2 * SPECTRA, feed_dev), jnp.bfloat16),
        in_specs=[frame_spec(a) for a in range(STEP)]
        + [whole(even_w.shape), whole(odd_w.shape)]
        + [whole((chans, 2, feed_dev)), whole(turn.shape)],
        out_specs=pl.BlockSpec(memory_space=pl.ANY),
        scratch_shapes=[
            pltpu.VMEM((STEP * feed_dev, half), jnp.bfloat16),
            pltpu.VMEM((STEP * feed_dev, half), jnp.bfloat16),
            pltpu.VMEM((depth, feed_dev, LANES), jnp.float32),
            pltpu.VMEM((depth, feed_dev, LANES), jnp.float32),
            pltpu.VMEM((chans * 2 * STEP, LANES), jnp.float32),
            pltpu.VMEM((chunks, chans, 2 * STEP, LANES), jnp.bfloat16),
            pltpu.SemaphoreType.DMA((chunks, rows)),
            pltpu.SemaphoreType.DMA((chunks, rows)),
            pltpu.SemaphoreType.DMA((chunks,)),
            pltpu.SemaphoreType.DMA((chunks,)),
            pltpu.SemaphoreType.DMA((chunks,)),
        ],
        compiler_params=pltpu.CompilerParams(
            collective_id=0,
            has_side_effects=True,
            vmem_limit_bytes=56 << 20,
            dimension_semantics=("arbitrary",),
        ),
        name="channelize",
    )(
        *([voltages] * STEP),
        jnp.asarray(even_w),
        jnp.asarray(odd_w),
        jnp.transpose(gains, (1, 2, 0)),
        jnp.asarray(turn),
    )


def correlate_kernel(spectra, out, wide_rows):
    _, rows, cols, depth, feed_dev = spectra.shape
    nq = FEEDS // (wide_rows.shape[1] // PITCH)
    step = jnp.minimum(pl.program_id(0), pl.num_programs(0) - 2)
    q = lax.rem(step, nq)
    slot = lax.rem(pl.program_id(0), 2)
    iblock = wide_rows.shape[1] // PITCH
    parts = out.shape[1] // iblock // 2
    jblocks = rows * cols // lax.axis_size("col")
    iblocks = iblock // feed_dev
    col = lax.axis_index("col")
    wide = MXU // LANES

    lefts = []
    for b in range(iblocks):
        at = q * iblocks + b
        y = spectra[0, lax.div(at, cols), lax.rem(at, cols)].astype(jnp.float32)
        z = y.reshape(depth // (2 * STEP), 2, STEP, feed_dev)
        z = jnp.concatenate([z[:, 1:], -z[:, :1]], axis=1).reshape(depth, feed_dev)
        lefts.append([y.T.astype(jnp.bfloat16), z.T.astype(jnp.bfloat16)])
    lefts = [jnp.concatenate(x, axis=0) for x in zip(*lefts)]
    rights = []
    for g in range(parts // wide):
        side = []
        for t in range(wide):
            at = col * jblocks + g * wide + t
            side.append(spectra[0, lax.div(at, cols), lax.rem(at, cols)])
        rights.append(jnp.concatenate(side, axis=1))

    pieces = 2 * (parts // wide)
    share = iblock // pieces
    for g in range(parts // wide):
        for p in (0, 1):
            product = jnp.dot(lefts[p], rights[g], preferred_element_type=jnp.float32)
            for t in range(wide):
                at = 2 * (g * wide + t) + p
                cut = product[:, t * LANES : (t + 1) * LANES]
                wide_rows[slot, pl.ds(at, iblock, stride=PITCH), :] = cut
            for r in range((2 * g + p) * share, (2 * g + p + 1) * share):
                rows_of = wide_rows[1 - slot, pl.ds(r * PITCH + lax.div(q, nq), 2 * parts), :]
                out[0, r * 2 * parts : (r + 1) * 2 * parts, :] = rows_of.astype(jnp.bfloat16)


def correlate(spectra):
    pairs, rows, cols, depth, feed_dev = spectra.shape
    jblock = FEEDS // cols
    iblock = 4 * feed_dev
    parts = jblock // LANES
    nq = FEEDS // iblock
    steps = pairs * nq

    def taken(n):
        return (jnp.minimum(n, steps - 1) // nq, 0, 0, 0, 0)

    def given(n):
        before = jnp.maximum(n - 1, 0)
        return (before // nq, before % nq, 0)

    flat = pl.pallas_call(
        correlate_kernel,
        grid=(steps + 1,),
        out_shape=jax.ShapeDtypeStruct((pairs, FEEDS * 2 * parts, LANES), jnp.bfloat16),
        in_specs=[pl.BlockSpec((1, rows, cols, depth, feed_dev), taken)],
        out_specs=pl.BlockSpec((1, iblock * 2 * parts, LANES), given),
        scratch_shapes=[pltpu.VMEM((2, iblock * PITCH, LANES), jnp.float32)],
        compiler_params=pltpu.CompilerParams(
            vmem_limit_bytes=63 << 20, dimension_semantics=("arbitrary",)
        ),
        name="correlate",
    )(spectra)
    flat = flat.reshape(pairs, FEEDS, parts, 2, LANES)
    return jnp.transpose(flat, (0, 1, 3, 2, 4)).reshape(pairs, FEEDS, 2, jblock)


def shards(voltages, gains):
    rows = lax.axis_size("row")
    cols = lax.axis_size("col")
    chans = gains.shape[1]
    fits = (
        voltages.shape[0] == LANES
        and rows * cols * LANES == FEEDS
        and cols == 2
        and FEEDS // cols // LANES == 8
        and chans % rows == 0
        and 4 * chans == LANES
        and voltages.shape[1] == (SPECTRA + TAPS - 1) * NFFT
    )
    if not fits:
        return plain_shards(voltages, gains)
    return correlate(channelize(voltages, gains))


def solution(mesh):
    placed = (P(("band", "row", "col"), None), P(("band", "row", "col"), None, None))
    return jax.shard_map(
        shards,
        mesh=mesh,
        in_specs=placed,
        out_specs=P(("band", "row"), None, None, "col"),
        check_vma=False,
    )
```

```python
import math

import jax
import jax.numpy as jnp
import ml_dtypes
import numpy as np
from jax import lax
from jax.experimental import pallas as pl
from jax.experimental.pallas import tpu as pltpu
from jax.sharding import PartitionSpec as P

FEEDS = 2048
NFFT = 2048
TAPS = 16
SPECTRA = 64
LANES = 128
STEP = 8
GROUP = 2
LAG = 2
WIDTH = 512
PITCH = 17
MESH = pl.DeviceIdType.MESH


def prototype(taps, length):
    total = taps * length
    index = jnp.arange(total).astype(jnp.float32)
    offset = (index - (total - 1) / 2.0) / length
    window = 0.5 - 0.5 * jnp.cos(2.0 * math.pi * (index + 0.5) / total)
    return (jnp.sinc(offset) * window).reshape(taps, length)


def dft_table(length, chans, first):
    sample = jnp.arange(length)
    channel = first + jnp.arange(chans)
    phase = sample[:, None] * channel[None, :] % length
    angle = phase.astype(jnp.float32) * (2.0 * math.pi / length)
    return jnp.concatenate([jnp.cos(angle), -jnp.sin(angle)], axis=1).astype(jnp.bfloat16)


def plain_shards(voltages, gains):
    rows = lax.axis_size("row")
    cols = lax.axis_size("col")
    feed_dev = voltages.shape[0]
    chans = gains.shape[1]
    sub = max(1, rows // chans)
    pairs = chans * sub // rows
    iblock = FEEDS // sub
    jblock = FEEDS // cols
    window = prototype(TAPS, NFFT)
    table = dft_table(NFFT, chans, NFFT // 8)
    scale = float(NFFT) ** (-0.5)
    blocks = voltages.reshape(feed_dev, -1, NFFT)
    total = jnp.zeros((feed_dev, SPECTRA, NFFT), jnp.float32)
    for tap in range(TAPS):
        total = total + blocks[:, tap : tap + SPECTRA, :].astype(jnp.float32) * window[tap]
    filtered = total.astype(jnp.bfloat16)
    raw = (
        jnp.dot(
            filtered.reshape(feed_dev * SPECTRA, NFFT), table, preferred_element_type=jnp.float32
        )
        * scale
    )
    raw = raw.reshape(feed_dev, SPECTRA, 2 * chans)
    real_part = raw[:, :, :chans]
    imag_part = raw[:, :, chans:]
    gain_re = gains[:, None, :, 0]
    gain_im = gains[:, None, :, 1]
    out_re = gain_re * real_part - gain_im * imag_part
    out_im = gain_re * imag_part + gain_im * real_part
    stacked = jnp.stack([out_re, out_im], axis=0)
    spectra = (
        jnp.transpose(stacked, (3, 1, 0, 2))
        .reshape(chans, feed_dev, 2 * SPECTRA)
        .astype(jnp.bfloat16)
    )
    outgoing = jnp.repeat(spectra, sub, axis=0)
    turned = lax.all_to_all(outgoing, "row", split_axis=0, concat_axis=1, tiled=True)
    turned = turned.reshape(pairs, rows, feed_dev, 2 * SPECTRA)
    gathered = lax.all_gather(turned, "col", axis=2, tiled=True)
    gathered = gathered.reshape(pairs, FEEDS, 2 * SPECTRA)
    pair_index = lax.axis_index("row") * pairs + jnp.arange(pairs)
    starts = pair_index % sub * iblock

    def first_rows(chan_rows, start):
        return lax.dynamic_slice_in_dim(chan_rows, start, iblock, 0)

    left = jax.vmap(first_rows)(gathered, starts)
    second = lax.dynamic_slice_in_dim(gathered, lax.axis_index("col") * jblock, jblock, 1)
    turned_second = jnp.concatenate([-second[:, :, SPECTRA:], second[:, :, :SPECTRA]], axis=2)
    right = jnp.concatenate([second, turned_second], axis=1)
    product = jnp.einsum("pis,pjs->pij", left, right, preferred_element_type=jnp.float32) / SPECTRA
    return product.astype(jnp.bfloat16).reshape(pairs, iblock, 2, jblock)


def folded_weights(chans, first):
    total = TAPS * NFFT
    m = np.arange(total)
    h = np.sinc((m - (total - 1) / 2.0) / NFFT) * (
        0.5 - 0.5 * np.cos(2.0 * np.pi * (m + 0.5) / total)
    )
    h = h.reshape(TAPS, NFFT)[:, : NFFT // 2]
    n = np.arange(NFFT // 2) - (NFFT - 1) / 2.0
    angle = 2.0 * np.pi / NFFT * n[:, None] * (first + np.arange(chans))[None, :]
    cos, sin = np.cos(angle), np.sin(angle)
    even, odd = [], []
    for u in range(TAPS // 2):
        plus = 0.5 * (h[u] + h[TAPS - 1 - u])[:, None]
        minus = 0.5 * (h[u] - h[TAPS - 1 - u])[:, None]
        even += [plus * cos, -minus * sin]
        odd += [minus * cos, -plus * sin]
    return [np.concatenate(x, axis=1).astype(ml_dtypes.bfloat16) for x in (even, odd)]


def rotation(chans, first):
    phase = -2.0 * np.pi / NFFT * (NFFT - 1) / 2.0 * (first + np.arange(chans))
    scale = NFFT**-0.5 * SPECTRA**-0.5
    turn = np.stack([np.cos(phase), np.sin(phase)], axis=1) * scale
    return np.repeat(turn[:, :, None], LANES, axis=2).astype(np.float32)


def channelize_kernel(rows, pairs, *refs):
    frames = refs[:STEP]
    even_w, odd_w, gains, turn, out, even, odd, low_acc, high_acc, stage, ready = refs[STEP : STEP + 11]
    send_sem, recv_sem, own_sem, pass_sem, passed_sem = refs[STEP + 11 :]
    i = pl.program_id(0)
    steps = pl.num_programs(0)
    feed_dev = frames[0].shape[0]
    half = NFFT // 2
    band, row, col = lax.axis_index("band"), lax.axis_index("row"), lax.axis_index("col")
    chunks = SPECTRA // STEP
    chans = rows * pairs
    delay = TAPS // STEP

    def to_row(ch, d):
        dest = lax.rem(row + d, rows)
        return pltpu.make_async_remote_copy(
            src_ref=ready.at[ch, pl.ds(dest * pairs, pairs)],
            dst_ref=out.at[:, row, col, pl.ds(pl.multiple_of(ch * 2 * STEP, 2 * STEP), 2 * STEP), :],
            send_sem=send_sem.at[ch, d],
            recv_sem=recv_sem.at[ch, d],
            device_id=(band, dest, col),
            device_id_type=MESH,
        )

    def from_row(ch, d):
        src = lax.rem(row + rows - d, rows)
        return pltpu.make_async_remote_copy(
            src_ref=ready.at[ch, pl.ds(src * pairs, pairs)],
            dst_ref=out.at[:, src, col, pl.ds(pl.multiple_of(ch * 2 * STEP, 2 * STEP), 2 * STEP), :],
            send_sem=send_sem.at[ch, d],
            recv_sem=recv_sem.at[ch, d],
            device_id=(band, src, col),
            device_id_type=MESH,
        )

    def own(ch):
        return pltpu.make_async_copy(
            ready.at[ch, pl.ds(row * pairs, pairs)],
            out.at[:, row, col, pl.ds(pl.multiple_of(ch * 2 * STEP, 2 * STEP), 2 * STEP), :],
            own_sem.at[ch],
        )

    def to_sibling(ch, c):
        block = out.at[:, :, c, pl.ds(pl.multiple_of(ch * 2 * STEP, 2 * STEP), 2 * STEP), :]
        return pltpu.make_async_remote_copy(
            src_ref=block,
            dst_ref=block,
            send_sem=pass_sem.at[ch],
            recv_sem=passed_sem.at[ch],
            device_id=(band, row, 1 - col),
            device_id_type=MESH,
        )

    def hand_on(ch):
        own(ch).wait()
        for d in range(1, rows):
            from_row(ch, d).wait_recv()
        to_sibling(ch, col).start()

    barrier = pltpu.get_barrier_semaphore()

    @pl.when(i == 0)
    def _():
        for d in range(1, rows):
            pl.semaphore_signal(
                barrier, inc=1, device_id=(band, lax.rem(row + d, rows), col), device_id_type=MESH
            )
        pl.semaphore_signal(barrier, inc=1, device_id=(band, row, 1 - col), device_id_type=MESH)
        low_acc[...] = jnp.zeros_like(low_acc)
        high_acc[...] = jnp.zeros_like(high_acc)

    back = LANES - 1 - lax.broadcasted_iota(jnp.int32, (GROUP * feed_dev, LANES), 1)

    def fold(first):
        group = frames[first : first + GROUP]
        span = slice(first * feed_dev, (first + GROUP) * feed_dev)
        for m in range(half // LANES):
            tail = jnp.concatenate(
                [f[:, NFFT - (m + 1) * LANES : NFFT - m * LANES] for f in group], axis=0
            ).astype(jnp.float32)
            tail = jnp.take_along_axis(tail, back, axis=1, mode="promise_in_bounds")
            tail = tail.astype(jnp.bfloat16)
            head = jnp.concatenate([f[:, m * LANES : (m + 1) * LANES] for f in group], axis=0)
            even[span, m * LANES : (m + 1) * LANES] = head + tail
            odd[span, m * LANES : (m + 1) * LANES] = head - tail

    fold(0)
    for first in range(0, STEP, GROUP):
        span = slice(first * feed_dev, (first + GROUP) * feed_dev)
        for q in range(TAPS * chans // WIDTH):
            cols = slice(q * WIDTH, (q + 1) * WIDTH)
            ge = jnp.dot(even[span], even_w[:, cols], preferred_element_type=jnp.float32)
            go = jnp.dot(odd[span], odd_w[:, cols], preferred_element_type=jnp.float32)
            if q == 0 and first + GROUP < STEP:
                fold(first + GROUP)
            low = ge + go
            high = ge - go
            for t in range(WIDTH // LANES):
                j = q * (WIDTH // LANES) + t
                cut = slice(t * LANES, (t + 1) * LANES)
                at = pl.ds(i * STEP + STEP - 2 - 2 * j + first, GROUP)
                low_acc[at] += low[:, cut].reshape(GROUP, feed_dev, LANES)
                at = pl.ds(i * STEP + 2 * j + first, GROUP)
                high_acc[at] += high[:, cut].reshape(GROUP, feed_dev, LANES)

    @pl.when(i == delay)
    def _():
        pl.semaphore_wait(barrier, rows)

    @pl.when(i >= delay)
    def _():
        ch = i - delay
        s0 = ch * STEP
        lane = lax.broadcasted_iota(jnp.int32, (feed_dev, LANES), 1)
        first = lane < LANES // 2
        sign = jnp.where(lax.rem(lane, 2 * chans) < chans, 1.0, -1.0).astype(jnp.float32)
        turn_re, turn_im = turn[:, 0, :], turn[:, 1, :]
        own_re, own_im = gains[:, 0, :], gains[:, 1, :]
        gain_re = own_re * turn_re - own_im * turn_im
        gain_im = own_re * turn_im + own_im * turn_re
        for s in range(0, STEP, 2):
            a = [low_acc[s0 + STEP - 1 + s + e] + sign * high_acc[s0 + 2 * STEP + s + e] for e in (0, 1)]
            b = [low_acc[s0 + STEP + s + e] + sign * high_acc[s0 + 2 * STEP - 1 + s + e] for e in (0, 1)]
            mine = jnp.where(first, a[0], b[1])
            other = jnp.where(first, a[1], b[0])
            both = (mine + pltpu.roll(other, LANES // 2, 1)).T
            for e in (0, 1):
                re = both[2 * chans * e : 2 * chans * e + chans]
                im = both[2 * chans * e + chans : 2 * chans * (e + 1)]
                stage[pl.ds(s + e, chans, stride=2 * STEP), :] = gain_re * re - gain_im * im
                stage[pl.ds(STEP + s + e, chans, stride=2 * STEP), :] = gain_re * im + gain_im * re
        ready[ch] = stage[...].reshape(chans, 2 * STEP, LANES).astype(jnp.bfloat16)
        for d in range(1, rows):
            to_row(ch, d).start()
        own(ch).start()

    @pl.when(i >= delay + LAG)
    def _():
        hand_on(i - delay - LAG)

    @pl.when(i == steps - 1)
    def _():
        for ch in range(chunks - LAG, chunks):
            hand_on(ch)

        @pl.loop(0, chunks)
        def _(ch):
            for d in range(1, rows):
                to_row(ch, d).wait_send()
            to_sibling(ch, col).wait_send()
            to_sibling(ch, 1 - col).wait_recv()


def channelize(voltages, gains):
    rows = lax.axis_size("row")
    cols = lax.axis_size("col")
    feed_dev, samples = voltages.shape
    chans = gains.shape[1]
    pairs = chans // rows
    frames = samples // NFFT
    steps = (frames + 1) // STEP
    half = NFFT // 2
    chunks = SPECTRA // STEP
    even_w, odd_w = folded_weights(chans, NFFT // 8)
    turn = rotation(chans, NFFT // 8)

    def frame_spec(a):
        return pl.BlockSpec((feed_dev, NFFT), lambda i: (0, jnp.maximum(i * STEP + a - 1, 0)))

    def whole(shape):
        return pl.BlockSpec(shape, lambda i: (0,) * len(shape))

    depth = steps * STEP + STEP

    def kernel(*refs):
        channelize_kernel(rows, pairs, *refs)

    return pl.pallas_call(
        kernel,
        grid=(steps,),
        out_shape=jax.ShapeDtypeStruct((pairs, rows, cols, 2 * SPECTRA, feed_dev), jnp.bfloat16),
        in_specs=[frame_spec(a) for a in range(STEP)]
        + [whole(even_w.shape), whole(odd_w.shape)]
        + [whole((chans, 2, feed_dev)), whole(turn.shape)],
        out_specs=pl.BlockSpec(memory_space=pl.ANY),
        scratch_shapes=[
            pltpu.VMEM((STEP * feed_dev, half), jnp.bfloat16),
            pltpu.VMEM((STEP * feed_dev, half), jnp.bfloat16),
            pltpu.VMEM((depth, feed_dev, LANES), jnp.float32),
            pltpu.VMEM((depth, feed_dev, LANES), jnp.float32),
            pltpu.VMEM((chans * 2 * STEP, LANES), jnp.float32),
            pltpu.VMEM((chunks, chans, 2 * STEP, LANES), jnp.bfloat16),
            pltpu.SemaphoreType.DMA((chunks, rows)),
            pltpu.SemaphoreType.DMA((chunks, rows)),
            pltpu.SemaphoreType.DMA((chunks,)),
            pltpu.SemaphoreType.DMA((chunks,)),
            pltpu.SemaphoreType.DMA((chunks,)),
        ],
        compiler_params=pltpu.CompilerParams(
            collective_id=0,
            has_side_effects=True,
            vmem_limit_bytes=56 << 20,
            dimension_semantics=("arbitrary",),
        ),
        name="channelize",
    )(
        *([voltages] * STEP),
        jnp.asarray(even_w),
        jnp.asarray(odd_w),
        jnp.transpose(gains, (1, 2, 0)),
        jnp.asarray(turn),
    )


def correlate_kernel(spectra, out, wide_rows):
    _, rows, cols, depth, feed_dev = spectra.shape
    nq = FEEDS // (wide_rows.shape[1] // PITCH)
    step = jnp.minimum(pl.program_id(0), pl.num_programs(0) - 2)
    q = lax.rem(step, nq)
    slot = lax.rem(pl.program_id(0), 2)
    iblock = wide_rows.shape[1] // PITCH
    parts = out.shape[1] // iblock // 2
    jblocks = rows * cols // lax.axis_size("col")
    iblocks = iblock // feed_dev
    col = lax.axis_index("col")
    wide = WIDTH // LANES

    lefts = []
    for b in range(iblocks):
        at = q * iblocks + b
        y = spectra[0, lax.div(at, cols), lax.rem(at, cols)].astype(jnp.float32)
        z = y.reshape(depth // (2 * STEP), 2, STEP, feed_dev)
        z = jnp.concatenate([z[:, 1:], -z[:, :1]], axis=1).reshape(depth, feed_dev)
        lefts.append([y.T.astype(jnp.bfloat16), z.T.astype(jnp.bfloat16)])
    lefts = [jnp.concatenate(x, axis=0) for x in zip(*lefts)]
    rights = []
    for g in range(parts // wide):
        side = []
        for t in range(wide):
            at = col * jblocks + g * wide + t
            side.append(spectra[0, lax.div(at, cols), lax.rem(at, cols)])
        rights.append(jnp.concatenate(side, axis=1))

    pieces = 2 * (parts // wide)
    share = iblock // pieces
    for g in range(parts // wide):
        for p in (0, 1):
            product = jnp.dot(lefts[p], rights[g], preferred_element_type=jnp.float32)
            for t in range(wide):
                at = 2 * (g * wide + t) + p
                cut = product[:, t * LANES : (t + 1) * LANES]
                wide_rows[slot, pl.ds(at, iblock, stride=PITCH), :] = cut
            for r in range((2 * g + p) * share, (2 * g + p + 1) * share):
                rows_of = wide_rows[1 - slot, pl.ds(r * PITCH + lax.div(q, nq), 2 * parts), :]
                out[0, r * 2 * parts : (r + 1) * 2 * parts, :] = rows_of.astype(jnp.bfloat16)


def correlate(spectra):
    pairs, rows, cols, depth, feed_dev = spectra.shape
    jblock = FEEDS // cols
    iblock = 4 * feed_dev
    parts = jblock // LANES
    nq = FEEDS // iblock
    steps = pairs * nq

    def taken(n):
        return (jnp.minimum(n, steps - 1) // nq, 0, 0, 0, 0)

    def given(n):
        before = jnp.maximum(n - 1, 0)
        return (before // nq, before % nq, 0)

    flat = pl.pallas_call(
        correlate_kernel,
        grid=(steps + 1,),
        out_shape=jax.ShapeDtypeStruct((pairs, FEEDS * 2 * parts, LANES), jnp.bfloat16),
        in_specs=[pl.BlockSpec((1, rows, cols, depth, feed_dev), taken)],
        out_specs=pl.BlockSpec((1, iblock * 2 * parts, LANES), given),
        scratch_shapes=[pltpu.VMEM((2, iblock * PITCH, LANES), jnp.float32)],
        compiler_params=pltpu.CompilerParams(
            vmem_limit_bytes=63 << 20, dimension_semantics=("arbitrary",)
        ),
        name="correlate",
    )(spectra)
    flat = flat.reshape(pairs, FEEDS, parts, 2, LANES)
    return jnp.transpose(flat, (0, 1, 3, 2, 4)).reshape(pairs, FEEDS, 2, jblock)


def shards(voltages, gains):
    rows = lax.axis_size("row")
    cols = lax.axis_size("col")
    chans = gains.shape[1]
    fits = (
        voltages.shape[0] == LANES
        and rows * cols * LANES == FEEDS
        and cols == 2
        and FEEDS // cols // LANES == 8
        and chans % rows == 0
        and 4 * chans == LANES
        and voltages.shape[1] == (SPECTRA + TAPS - 1) * NFFT
    )
    if not fits:
        return plain_shards(voltages, gains)
    return correlate(channelize(voltages, gains))


def solution(mesh):
    placed = (P(("band", "row", "col"), None), P(("band", "row", "col"), None, None))
    return jax.shard_map(
        shards,
        mesh=mesh,
        in_specs=placed,
        out_specs=P(("band", "row"), None, None, "col"),
        check_vma=False,
    )
```
